128 devices in a mesh: dp: 8 (over y, z_hi), tensor: 16 (over z_lo, x, core).
Axes of the slice: x: 4, y: 4, z: 4 (z_hi: 2, z_lo: 2; z = z_hi * 2 + z_lo), core: 2. Of those that a mesh axis runs over, the one named last changes fastest.
Arguments:
- inputs: bfloat16 [12288, 8192], P('dp', 'tensor'), may hold values from -6 to 6
- grad_out: bfloat16 [2, 12288, 22016], P(None, 'dp', 'tensor'), may hold values from -0.0068359375 to 0.0068359375
- basis: bfloat16 [2, 8192, 128], replicated, may hold values from -0.5 to 0.5
- first_moment: float32 [2, 128, 16, 1376], P(None, None, 'tensor', 'dp'), may hold values from -4 to 4
- second_moment: float32 [2, 128, 16, 1376], P(None, None, 'tensor', 'dp'), may hold values from 0.002 to 0.05
Outputs:
- update: bfloat16 [2, 8192, 22016], P(None, 'dp', 'tensor')
- new_first: float32 [2, 128, 16, 1376], P(None, None, 'tensor', 'dp')
- new_second: float32 [2, 128, 16, 1376], P(None, None, 'tensor', 'dp')
The draws below stay inside these ranges and needn't reach their ends.
All inputs are finite; a program needn't handle non-finite values.
Results may differ from the reference program's by a relative error of at most 0.005.
Values may be sent and summed in bfloat16 or wider, within the bound.
No kernel may reach another device: no remote copies, remote signals or barrier semaphores. Data moves between devices by JAX's collectives and lax.ppermute only.
A program may use at most 64 MiB of HBM per device.

```python
import math
import jax
import jax.numpy as jnp

D = 8192
FF = 22016
R = 128
STEP = 10
TOKENS = 12288
N_TENSOR = 16


def level_of(rng, dims, pieces, low, top_value):
    def one(axis_at, blocks):
        draws = jax.random.uniform(jax.random.fold_in(jax.random.fold_in(rng, 6), axis_at), (blocks,), jnp.float32, low / len(pieces), top_value / len(pieces))
        return jnp.repeat(jnp.exp(draws), dims[axis_at] // blocks).reshape((-1,) + (1,) * (len(dims) - axis_at - 1))

    factor_of = one(*pieces[0])
    for cut in pieces[1:]:
        factor_of = factor_of * one(*cut)
    return factor_of


def scatter_about(stream_key, shape, width, most, shards=(), dtype=jnp.bfloat16):
    values = jax.random.normal(stream_key, shape, jnp.float32) * width
    if len(shards) > 0:
        values = level_of(stream_key, shape, shards, -0.22, 0.18) * values
    return jnp.clip(values, min=-most, max=most).astype(dtype)


def setup_inputs(seed: int = 0) -> dict:
    seeds = jax.random.split(jax.random.key(seed), 6)
    return {
        "inputs": scatter_about(seeds[0], (TOKENS, D), 1.0, 6.0, ((0, 8), (1, 16))),
        "grad_out": scatter_about(seeds[1], (2, TOKENS, FF), (TOKENS * D // R) ** -0.5, 0.0068359375, ((1, 8), (2, 16))),
        "basis": scatter_about(seeds[2], (2, D, R), R ** -0.5, 0.5),
        "first_moment": scatter_about(seeds[3], (2, R, N_TENSOR, FF // N_TENSOR), 0.5, 4.0, ((2, 16), (3, 8)), jnp.float32),
        "second_moment": jnp.clip(jnp.exp(math.log(0.05) - 3.218876 * jax.random.uniform(seeds[4], (2, R, N_TENSOR, FF // N_TENSOR), jnp.float32) ** level_of(seeds[4], (2, R, N_TENSOR, FF // N_TENSOR), ((2, 16), (3, 8)), -0.2, 0.2)), 0.002, 0.05),
    }


beta_one = 0.9
beta_two = 0.999
epsilon = 1e-08

def reference(inputs, grad_out, basis, first_moment, second_moment):

    def project(index):
        return jnp.dot(inputs, basis[index], preferred_element_type=jnp.float32).astype(jnp.bfloat16)
    projected = [project(0), project(1)]
    rank_grad = jnp.stack([jnp.dot(projected[g].T, grad_out[g], preferred_element_type=jnp.float32) for g in range(2)])
    rank_grad = rank_grad.reshape(first_moment.shape)
    new_first = beta_one * first_moment + (1.0 - beta_one) * rank_grad
    new_second = beta_two * second_moment + (1.0 - beta_two) * rank_grad * rank_grad
    corr_one = 1.0 - beta_one ** STEP
    corr_two = 1.0 - beta_two ** STEP
    normalized = (new_first / corr_one / (jnp.sqrt(new_second / corr_two) + epsilon)).astype(jnp.bfloat16)
    flat = normalized.reshape(2, R, FF)
    update = jnp.stack([jnp.dot(basis[g], flat[g], preferred_element_type=jnp.float32).astype(jnp.bfloat16) for g in range(2)])
    return (update, new_first, new_second)
```

```python
import functools

import jax
import jax.numpy as jnp
from jax import lax
from jax.experimental import pallas as pl
from jax.experimental.pallas import tpu as pltpu
from jax.sharding import PartitionSpec as P

STEP = 10

beta_one = 0.9
beta_two = 0.999
epsilon = 1e-08
corr_one = 1.0 - beta_one**STEP
corr_two = 1.0 - beta_two**STEP

NX, NY = 4, 4
CHAINS = ((0, 1),)

F32, BF16 = jnp.float32, jnp.bfloat16
NT = (((1,), (1,)), ((), ()))


def to_core(v):
    return lax.ppermute(v, "tensor", [(i, i ^ 1) for i in range(16)])


def to_x(v, k):
    pairs = [(i, (i & 9) | ((((i >> 1) + k) & 3) << 1)) for i in range(16)]
    return lax.ppermute(v, "tensor", pairs)


def to_zlo(v):
    return lax.ppermute(v, "tensor", [(i, i ^ 8) for i in range(16)])


def to_y(v, k):
    return lax.ppermute(v, "dp", [(i, (i & 1) | ((((i >> 1) + k) & 3) << 1)) for i in range(8)])


def to_zhi(v):
    return lax.ppermute(v, "dp", [(i, i ^ 1) for i in range(8)])


def params(mib=24):
    return pltpu.CompilerParams(vmem_limit_bytes=mib * 2**20)


def project_kernel(pos, inputs_ref, *refs):
    basis_refs, send_ref, own_ref = refs[:-2], refs[-2], refs[-1]
    step = pl.program_id(0)
    product = [
        jnp.dot(inputs_ref[...], ref[0], preferred_element_type=F32) for ref in basis_refs
    ]
    product = jnp.concatenate(product, axis=1) if len(product) > 1 else product[0]

    @pl.when(step < NX)
    def _():
        send_ref[...] = product.astype(BF16)

    @pl.when(step >= NX)
    def _():
        own_ref[...] = product


def project(pos, inputs, basis, chain):
    tokens, feat = inputs.shape
    rank = basis.shape[2]
    piece = tokens // (2 * NX)
    width = rank * len(chain)

    def rows(s, pos):
        core = jnp.where(s < NX, 1 - pos[0], pos[0])
        return core * NX + lax.rem(pos[1] + lax.rem(s, NX), NX)

    return pl.pallas_call(
        project_kernel,
        grid_spec=pltpu.PrefetchScalarGridSpec(
            num_scalar_prefetch=1,
            grid=(2 * NX,),
            in_specs=[pl.BlockSpec((piece, feat), lambda s, pos: (rows(s, pos), 0))]
            + [
                pl.BlockSpec((1, feat, rank), lambda s, pos, g=g: (g, 0, 0)) for g in chain
            ],
            out_specs=[
                pl.BlockSpec((piece, width), lambda s, pos: (jnp.minimum(s, NX - 1), 0)),
                pl.BlockSpec((piece, width), lambda s, pos: (jnp.maximum(s - NX, 0), 0)),
            ],
        ),
        out_shape=[
            jax.ShapeDtypeStruct((NX * piece, width), BF16),
            jax.ShapeDtypeStruct((NX * piece, width), F32),
        ],
        compiler_params=params(),
        name="project",
    )(pos, inputs, *([basis] * len(chain)))


BLOCK = 352


def rank_kernel(chain, steps, pos, mine_ref, theirs_ref, grad_ref, own_ref, *refs):
    outs, proj, total = refs[:-2], refs[-2], refs[-1]
    g, step = pl.program_id(0), pl.program_id(1)
    piece = mine_ref.shape[0] // NX

    @pl.when((g == 0) & (step == 0))
    def _():
        for k in range(NX):
            x = lax.rem(pos[1] - k + NX, NX)
            for ref, core in ((mine_ref, pos[0]), (theirs_ref, 1 - pos[0])):
                at = pl.multiple_of((core * NX + x) * piece, piece)
                for h in range(len(chain)):
                    proj[h, pl.ds(at, piece), :] = ref[
                        k * piece : (k + 1) * piece, h * 128 : (h + 1) * 128
                    ]

    total[pl.ds(pl.multiple_of(step * BLOCK, BLOCK), BLOCK), :] = jnp.dot(
        grad_ref[0], proj[g], preferred_element_type=F32
    )

    @pl.when(step == steps - 1)
    def _():
        share = own_ref.shape[1]
        for k in range(NY):
            y = lax.rem(pos[2] + k, NY)
            part = total[pl.ds(pl.multiple_of(y * share, 8), share), :]
            if k == 0:
                own_ref[g] = part
            else:
                outs[k - 1][g] = part.astype(BF16)


def rank_grad(pos, mine, theirs, grad_t, chain):
    n = len(chain)
    cols, tokens = grad_t.shape[1:]
    rank = mine.shape[1] // n
    share = cols // NY
    steps = pl.cdiv(cols, BLOCK)
    whole = lambda g, s, pos: (0, 0, 0)
    return pl.pallas_call(
        functools.partial(rank_kernel, chain, steps),
        grid_spec=pltpu.PrefetchScalarGridSpec(
            num_scalar_prefetch=1,
            grid=(n, steps),
            in_specs=[
                pl.BlockSpec(mine.shape, lambda g, s, pos: (0, 0)),
                pl.BlockSpec(theirs.shape, lambda g, s, pos: (0, 0)),
                pl.BlockSpec((1, BLOCK, tokens), lambda g, s, pos: (g + chain[0], s, 0)),
            ],
            out_specs=[pl.BlockSpec((n, share, rank), whole)] * NY,
            scratch_shapes=[
                pltpu.VMEM((n, tokens, rank), BF16),
                pltpu.VMEM((steps * BLOCK, rank), F32),
            ],
        ),
        out_shape=[jax.ShapeDtypeStruct((n, share, rank), F32)]
        + [jax.ShapeDtypeStruct((n, share, rank), BF16)] * (NY - 1),
        compiler_params=params(),
        name="rank_grad",
    )(pos, mine, theirs, grad_t)


def adam_kernel(
    chain, pos, own_ref, got_ref, first_ref, second_ref, far_first_ref, far_second_ref,
    norm_ref, new_first_ref, new_second_ref,
):
    low = pos[3] == 0
    half = own_ref.shape[1] // 2
    for h, g in enumerate(chain):
        rows = slice(g * half, (g + 1) * half)
        grad = own_ref[h] + got_ref[h].astype(F32)

        def both(near, far):
            near, far = near[rows, :], far[rows, :]
            return jnp.concatenate(
                [jnp.where(low, near, far), jnp.where(low, far, near)], axis=0
            )

        new_first = beta_one * both(first_ref, far_first_ref) + (1.0 - beta_one) * grad
        new_second = beta_two * both(second_ref, far_second_ref) + (1.0 - beta_two) * grad * grad
        norm_ref[h] = (
            new_first / corr_one / (jnp.sqrt(new_second / corr_two) + epsilon)
        ).astype(BF16)
        to = slice(h * half, (h + 1) * half)
        new_first_ref[to, :] = jnp.where(low, new_first[:half], new_first[half:])
        new_second_ref[to, :] = jnp.where(low, new_second[:half], new_second[half:])


def adam(pos, own, got, first, second, far_first, far_second, chain):
    n, share, rank = own.shape
    vmem = pl.BlockSpec(memory_space=pltpu.VMEM)
    return pl.pallas_call(
        functools.partial(adam_kernel, chain),
        in_specs=[pl.BlockSpec(memory_space=pltpu.SMEM)] + [vmem] * 6,
        out_specs=[vmem] * 3,
        out_shape=[jax.ShapeDtypeStruct((n, share, rank), BF16)]
        + [jax.ShapeDtypeStruct((n * share // 2, rank), F32)] * 2,
        compiler_params=params(),
        name="adam",
    )(pos, own, got, first, second, far_first, far_second)


def update_kernel(n, pos, *refs):
    pieces, basis_ref, out_ref, wide, norm = refs[: NY * n], *refs[NY * n :]
    g, step = pl.program_id(0), pl.program_id(1)
    share = pieces[0].shape[1]
    rows = out_ref.shape[1]

    for h in range(n):

        @pl.when((g == h) & (step == 0))
        def _():
            for k in range(NY):
                y = lax.rem(pos[2] - k + NY, NY)
                at = pl.multiple_of(y * share, 8)
                wide[pl.ds(at, share), :] = pieces[h * NY + k][0].astype(F32)
            norm[...] = wide[...].astype(BF16)

    at = pl.multiple_of(step * rows, rows)
    out_ref[0] = lax.dot_general(
        norm[pl.ds(at, rows), :], basis_ref[0], NT, preferred_element_type=F32
    ).astype(BF16)


def update(pos, pieces, basis, cols, weight_rows):
    n = len(pieces)
    flat = [p for per_g in pieces for p in per_g]
    share, rank = flat[0][0].shape[1:]
    rows = cols // 2
    return pl.pallas_call(
        functools.partial(update_kernel, n),
        grid_spec=pltpu.PrefetchScalarGridSpec(
            num_scalar_prefetch=1,
            grid=(n, cols // rows),
            in_specs=[
                pl.BlockSpec((1, share, rank), lambda g, s, pos, h=h: (h, 0, 0)) for _, h in flat
            ]
            + [pl.BlockSpec((1, weight_rows, rank), lambda g, s, pos: (g, 0, 0))],
            out_specs=pl.BlockSpec((1, rows, weight_rows), lambda g, s, pos: (g, s, 0)),
            scratch_shapes=[pltpu.VMEM((cols, rank), F32), pltpu.VMEM((cols, rank), BF16)],
        ),
        out_shape=jax.ShapeDtypeStruct((n, cols, weight_rows), BF16),
        compiler_params=params(),
        name="update",
    )(pos, *[a for a, _ in flat], basis)


def body(inputs, grad_out, basis, first_moment, second_moment):
    t, d = lax.axis_index("tensor"), lax.axis_index("dp")
    pos = jnp.stack([t & 1, (t >> 1) & 3, d >> 1, d & 1]).astype(jnp.int32)
    feat_rows, weight_rows = inputs.shape[1], basis.shape[1] // lax.axis_size("dp")
    feat_basis = lax.dynamic_slice_in_dim(basis, t * feat_rows, feat_rows, 1)
    row_basis = lax.dynamic_slice_in_dim(basis, d * weight_rows, weight_rows, 1)
    piece = inputs.shape[0] // (2 * NX)
    grad_t = jnp.transpose(grad_out, (0, 2, 1))
    cols = grad_t.shape[1]
    n_g, rank = first_moment.shape[:2]
    flat = lambda m: jnp.transpose(m, (0, 3, 2, 1)).reshape(-1, rank)
    first, second = flat(first_moment), flat(second_moment)
    far_first, far_second = to_zhi(first), to_zhi(second)

    norms, firsts, seconds = [], [], []
    for chain in CHAINS:
        send, own = project(pos, inputs, feat_basis, chain)
        got = to_core(send)
        part = lambda v, k: v[k * piece : (k + 1) * piece].astype(F32)
        sums = [part(own, k) + part(got, k) for k in range(NX)]
        total = sums[0]
        for k in range(1, NX):
            total = total + to_x(sums[k].astype(BF16), k).astype(F32)
        total = (total + to_zlo(total.astype(BF16)).astype(F32)).astype(BF16)
        mine = jnp.concatenate([total] + [to_x(total, k) for k in range(1, NX)], axis=0)
        theirs = to_core(mine)

        own, *others = rank_grad(pos, mine, theirs, grad_t, chain)
        for k in range(1, NY):
            own = own + to_y(others[k - 1], k).astype(F32)
        got = to_zhi(own.astype(BF16))
        norm, new_first, new_second = adam(
            pos, own, got, first, second, far_first, far_second, chain
        )
        gathered = [norm] + [to_y(norm, k) for k in range(1, NY)]
        norms += [[(v, h) for v in gathered] for h in range(len(chain))]
        firsts.append(new_first)
        seconds.append(new_second)

    out = jnp.transpose(update(pos, norms, row_basis, cols, weight_rows), (0, 2, 1))

    def shaped(parts):
        m = jnp.concatenate(parts, axis=0) if len(parts) > 1 else parts[0]
        return jnp.transpose(m.reshape(n_g, -1, 1, rank), (0, 3, 2, 1))

    return out, shaped(firsts), shaped(seconds)


def solution(mesh):
    in_specs = (
        P("dp", "tensor"),
        P(None, "dp", "tensor"),
        P(),
        P(None, None, "tensor", "dp"),
        P(None, None, "tensor", "dp"),
    )
    out_specs = (
        P(None, "dp", "tensor"),
        P(None, None, "tensor", "dp"),
        P(None, None, "tensor", "dp"),
    )
    return jax.shard_map(body, mesh=mesh, in_specs=in_specs, out_specs=out_specs, check_vma=False)
```

```python
import jax
import jax.numpy as jnp
from jax import lax
from jax.experimental import pallas as pl
from jax.experimental.pallas import tpu as pltpu
from jax.sharding import PartitionSpec as P

STEP = 10

beta_one = 0.9
beta_two = 0.999
epsilon = 1e-08
corr_one = 1.0 - beta_one**STEP
corr_two = 1.0 - beta_two**STEP

NX, NY = 4, 4

F32, BF16 = jnp.float32, jnp.bfloat16
HBM = pl.BlockSpec(memory_space=pltpu.HBM)
VMEM = pl.BlockSpec(memory_space=pltpu.VMEM)


def swap(v, axis, size, bits):
    return lax.ppermute(v, axis, [(i, i ^ bits) for i in range(size)])


def to_core(v):
    return swap(v, "tensor", 16, 1)


def to_x(v, k):
    return swap(v, "tensor", 16, k * 2)


def to_zlo(v):
    return swap(v, "tensor", 16, 8)


def to_y(v, k):
    return swap(v, "dp", 8, k * 2)


def to_zhi(v):
    return swap(v, "dp", 8, 1)


def place():
    t, d = lax.axis_index("tensor"), lax.axis_index("dp")
    return {"t": t, "core": t & 1, "x": (t >> 1) & 3, "y": d >> 1, "z": d & 1}


def params(mib):
    return pltpu.CompilerParams(vmem_limit_bytes=mib * 2**20)


def cost(flops, moved):
    return pl.CostEstimate(flops=flops, bytes_accessed=moved, transcendentals=0)


def project_kernel(
    inputs_ref, basis_ref, send_ref, own_ref, rows, basis, row_sem, basis_sem
):
    at = place()
    n_g, feat, rank = basis.shape
    half = rows.shape[1]
    piece = half // NX
    copies = []
    for g in range(n_g):
        src = basis_ref.at[g, pl.ds(pl.multiple_of(at["t"] * feat, feat), feat), :]
        copies.append(pltpu.make_async_copy(src, basis.at[g], basis_sem.at[g]))
    for h, core in enumerate((1 - at["core"], at["core"])):
        src = inputs_ref.at[pl.ds(pl.multiple_of(core * half, half), half), :]
        copies.append(pltpu.make_async_copy(src, rows.at[h], row_sem.at[h]))
    for copy in copies:
        copy.start()
    for copy in copies[:n_g]:
        copy.wait()
    both = jnp.concatenate([basis[g] for g in range(n_g)], axis=1)
    for h in range(2):
        copies[n_g + h].wait()
        for k in range(NX):
            src = pl.multiple_of((at["x"] ^ k) * piece, piece)
            product = jnp.dot(rows[h, pl.ds(src, piece), :], both, preferred_element_type=F32)
            to = slice(k * piece, (k + 1) * piece)
            if h == 0:
                send_ref[to, :] = product.astype(BF16)
            else:
                own_ref[to, :] = product


def project(inputs, basis):
    tokens, feat = inputs.shape
    n_g, _, rank = basis.shape
    half = tokens // 2
    return pl.pallas_call(
        project_kernel,
        in_specs=[HBM] * 2,
        out_specs=[VMEM] * 2,
        out_shape=[
            jax.ShapeDtypeStruct((half, n_g * rank), BF16),
            jax.ShapeDtypeStruct((half, n_g * rank), F32),
        ],
        scratch_shapes=[
            pltpu.VMEM((2, half, feat), BF16),
            pltpu.VMEM((n_g, feat, rank), BF16),
            pltpu.SemaphoreType.DMA((2,)),
            pltpu.SemaphoreType.DMA((n_g,)),
        ],
        compiler_params=params(52),
        cost_estimate=cost(2 * tokens * feat * n_g * rank, 2 * tokens * feat),
        name="project",
    )(inputs, basis)


def half_product(at, core, part_ref, grad_ref, proj, g):
    half = part_ref.shape[0]
    piece = half // NX
    rank = proj.shape[1]
    for k in range(NX):
        to = pl.multiple_of((at["x"] ^ k) * piece, piece)
        proj[pl.ds(to, piece), :] = part_ref[
            k * piece : (k + 1) * piece, g * rank : (g + 1) * rank
        ]
    tokens = pl.ds(pl.multiple_of(core * half, half), half)
    return jnp.dot(grad_ref[:, tokens], proj[...], preferred_element_type=F32)


def near_kernel(part_ref, *refs):
    grads, total_ref, proj = refs[:-2], refs[-2], refs[-1]
    at = place()
    for g, grad_ref in enumerate(grads):
        total_ref[g] = half_product(at, at["core"], part_ref, grad_ref, proj.at[g], g)


def rank_near(part, grads, rank):
    cols, tokens = grads[0].shape
    n_g = len(grads)
    return pl.pallas_call(
        near_kernel,
        in_specs=[VMEM] * (1 + n_g),
        out_specs=VMEM,
        out_shape=jax.ShapeDtypeStruct((n_g, cols, rank), F32),
        scratch_shapes=[pltpu.VMEM((n_g, tokens // 2, rank), BF16)],
        compiler_params=params(8),
        cost_estimate=cost(n_g * tokens * cols * rank, 4 * 2**20),
        name="rank_near",
    )(part, *grads)


def far_kernel(g, part_ref, near_ref, grad_ref, own_ref, *refs):
    outs, proj, total = refs[:-2], refs[-2], refs[-1]
    at = place()
    share = own_ref.shape[0]
    total[...] = near_ref[g] + half_product(at, 1 - at["core"], part_ref, grad_ref, proj, g)
    for k in range(NY):
        mine = total[pl.ds(pl.multiple_of((at["y"] ^ k) * share, 8), share), :]
        if k == 0:
            own_ref[...] = mine
        else:
            outs[k - 1][...] = mine.astype(BF16)


def rank_far(part, near, grad, g):
    cols, tokens = grad.shape
    rank = near.shape[2]
    share = cols // NY
    return pl.pallas_call(
        lambda *refs: far_kernel(g, *refs),
        in_specs=[VMEM] * 3,
        out_specs=[VMEM] * NY,
        out_shape=[jax.ShapeDtypeStruct((share, rank), F32)]
        + [jax.ShapeDtypeStruct((share, rank), BF16)] * (NY - 1),
        scratch_shapes=[pltpu.VMEM((tokens // 2, rank), BF16), pltpu.VMEM((cols, rank), F32)],
        compiler_params=params(8),
        cost_estimate=cost(tokens * cols * rank, 2 * 2**20),
        name="rank_far",
    )(part, near, grad)


def adam_kernel(n_g, *refs):
    owns, gots = refs[:n_g], refs[n_g : 2 * n_g]
    near_ref, far_ref, norm_ref, new_first_ref, new_second_ref = refs[2 * n_g :]
    low = place()["z"] == 0
    half = owns[0].shape[0] // 2
    for g in range(n_g):
        grad = owns[g][...] + gots[g][...].astype(F32)

        def moment(i):
            rows = slice((i * n_g + g) * half, (i * n_g + g + 1) * half)
            near, far = near_ref[rows, :], far_ref[rows, :]
            return jnp.concatenate(
                [jnp.where(low, near, far), jnp.where(low, far, near)], axis=0
            )

        new_first = beta_one * moment(0) + (1.0 - beta_one) * grad
        new_second = beta_two * moment(1) + (1.0 - beta_two) * grad * grad
        norm_ref[g] = (
            new_first / corr_one / (jnp.sqrt(new_second / corr_two) + epsilon)
        ).astype(BF16)
        rows = slice(g * half, (g + 1) * half)
        new_first_ref[rows, 0, :] = jnp.where(low, new_first[:half], new_first[half:])
        new_second_ref[rows, 0, :] = jnp.where(low, new_second[:half], new_second[half:])


def adam(owns, gots, moments, far_moments):
    n_g = len(owns)
    share, rank = owns[0].shape
    return pl.pallas_call(
        lambda *refs: adam_kernel(n_g, *refs),
        in_specs=[VMEM] * (2 * n_g + 2),
        out_specs=[VMEM] * 3,
        out_shape=[jax.ShapeDtypeStruct((n_g, share, rank), BF16)]
        + [jax.ShapeDtypeStruct((n_g * share // 2, 1, rank), F32)] * 2,
        compiler_params=params(8),
        name="adam",
    )(*owns, *gots, moments, far_moments)


BLOCK = 352


def update_kernel(first_half, even_ref, odd_ref, basis_ref, *refs):
    out_ref, wide, norm, block, sem = refs[-5:]
    y = place()["y"]
    pair = y >> 1 if first_half else 1 - (y >> 1)
    n_g, share, _ = even_ref.shape
    rows = 2 * share
    copies = []
    for g in range(n_g):
        for ref, parity in ((even_ref, y & 1), (odd_ref, 1 - (y & 1))):
            wide[g, pl.ds(pl.multiple_of(parity * share, 8), share), :] = ref[g].astype(F32)
        norm[g] = wide[g].astype(BF16)
        for i, start in enumerate(range(0, rows, BLOCK)):
            size = min(BLOCK, rows - start)
            block[g, start : start + size, :] = jnp.dot(
                norm[g, start : start + size, :], basis_ref[g], preferred_element_type=F32
            ).astype(BF16)
            copies.append(
                pltpu.make_async_copy(
                    block.at[g, start : start + size, :],
                    out_ref.at[g, pl.ds(pl.multiple_of(pair * rows + start, 16), size), :],
                    sem.at[g, i],
                )
            )
            copies[-1].start()
    for copy in copies:
        copy.wait()


def update(even, odd, basis_t, out):
    n_g, share, rank = even.shape
    weight_rows = basis_t.shape[2]
    return pl.pallas_call(
        lambda *refs: update_kernel(out is None, *refs),
        in_specs=[VMEM] * 3 + ([HBM] if out is not None else []),
        out_specs=HBM,
        out_shape=jax.ShapeDtypeStruct((n_g, share * NY, weight_rows), BF16),
        scratch_shapes=[
            pltpu.VMEM((n_g, 2 * share, rank), F32),
            pltpu.VMEM((n_g, 2 * share, rank), BF16),
            pltpu.VMEM((n_g, 2 * share, weight_rows), BF16),
            pltpu.SemaphoreType.DMA((n_g, pl.cdiv(2 * share, BLOCK))),
        ],
        input_output_aliases={} if out is None else {3: 0},
        compiler_params=params(12),
        cost_estimate=cost(4 * n_g * share * rank * weight_rows, 4 * n_g * share * weight_rows),
        name="update",
    )(even, odd, basis_t, *([] if out is None else [out]))


def body(inputs, grad_out, basis, first_moment, second_moment):
    weight_rows = basis.shape[1] // lax.axis_size("dp")
    row_basis = lax.dynamic_slice_in_dim(
        basis, lax.axis_index("dp") * weight_rows, weight_rows, 1
    )
    row_basis_t = jnp.transpose(row_basis, (0, 2, 1))
    piece = inputs.shape[0] // (2 * NX)
    grad_t = jnp.transpose(grad_out, (0, 2, 1))
    n_g, rank = first_moment.shape[:2]
    flat = lambda m: jnp.transpose(m, (0, 3, 2, 1)).reshape(-1, rank)
    send, own = project(inputs, basis)
    send, first, second = lax.optimization_barrier(
        (send, flat(first_moment), flat(second_moment))
    )
    moments = jnp.concatenate([first, second], axis=0)
    got = to_core(send)
    far_moments = to_zhi(moments)
    part = lambda v, k: v[k * piece : (k + 1) * piece].astype(F32)
    sums = [part(own, k) + part(got, k) for k in range(NX)]
    total = sums[0]
    for k in range(1, NX):
        total = total + to_x(sums[k].astype(BF16), k).astype(F32)
    total, far_moments, row_basis_t = lax.optimization_barrier(
        (total, far_moments, row_basis_t)
    )
    total = (total + to_zlo(total.astype(BF16)).astype(F32)).astype(BF16)
    near_part = jnp.concatenate([total] + [to_x(total, k) for k in range(1, NX)], axis=0)
    near_part, *grads = lax.optimization_barrier((near_part, *(grad_t[g] for g in range(n_g))))
    far_part = to_core(near_part)
    near = rank_near(near_part, grads, rank)
    far_part, near = lax.optimization_barrier((far_part, near))

    owns, gots = [], []
    for g in range(n_g):
        own, *others = rank_far(far_part, near, grads[g], g)
        for k in range(1, NY):
            own = own + to_y(others[k - 1], k).astype(F32)
        owns.append(own)
        gots.append(to_zhi(own.astype(BF16)))
    norm, new_first, new_second = adam(owns, gots, moments, far_moments)
    pieces = [norm] + [to_y(norm, k) for k in range(1, NY)]
    out = update(pieces[0], pieces[1], row_basis_t, None)
    out = update(pieces[2], pieces[3], row_basis_t, out)

    def shaped(m):
        return jnp.transpose(m.reshape(n_g, -1, 1, rank), (0, 3, 2, 1))

    return jnp.transpose(out, (0, 2, 1)), shaped(new_first), shaped(new_second)


def solution(mesh):
    in_specs = (
        P("dp", "tensor"),
        P(None, "dp", "tensor"),
        P(),
        P(None, None, "tensor", "dp"),
        P(None, None, "tensor", "dp"),
    )
    out_specs = (
        P(None, "dp", "tensor"),
        P(None, None, "tensor", "dp"),
        P(None, None, "tensor", "dp"),
    )
    return jax.shard_map(body, mesh=mesh, in_specs=in_specs, out_specs=out_specs, check_vma=False)
```

```python
import jax
import jax.numpy as jnp
from jax import lax
from jax.experimental import pallas as pl
from jax.experimental.pallas import tpu as pltpu
from jax.sharding import PartitionSpec as P

STEP = 10

beta_one = 0.9
beta_two = 0.999
epsilon = 1e-08
corr_one = 1.0 - beta_one**STEP
corr_two = 1.0 - beta_two**STEP

NX, NY = 4, 4
ORDER = (2, 1, 3)
STAGE_MIB = 48
AG_X, AG_Y = (2, 1, 3), (2, 1, 3)
PIECES = (0, 1, 3, 2)

F32, BF16 = jnp.float32, jnp.bfloat16
HBM = pl.BlockSpec(memory_space=pltpu.HBM)
VMEM = pl.BlockSpec(memory_space=pltpu.VMEM)


def swap(v, axis, size, bits):
    return lax.ppermute(v, axis, [(i, i ^ bits) for i in range(size)])


def to_core(v):
    return swap(v, "tensor", 16, 1)


def to_x(v, k):
    return swap(v, "tensor", 16, k * 2)


def to_zlo(v):
    return swap(v, "tensor", 16, 8)


def to_y(v, k):
    return swap(v, "dp", 8, k * 2)


def to_zhi(v):
    return swap(v, "dp", 8, 1)


def place():
    t, d = lax.axis_index("tensor"), lax.axis_index("dp")
    return {"t": t, "core": t & 1, "x": (t >> 1) & 3, "y": d >> 1, "z": d & 1}


def params(mib):
    return pltpu.CompilerParams(vmem_limit_bytes=mib * 2**20)


def cost(flops, moved):
    return pl.CostEstimate(flops=flops, bytes_accessed=moved, transcendentals=0)


def project_kernel(
    inputs_ref, basis_ref, send_ref, own_ref, rows, basis, row_sem, basis_sem
):
    at = place()
    n_g, feat, rank = basis.shape
    half = rows.shape[1]
    piece = half // NX
    copies = []
    for g in range(n_g):
        src = basis_ref.at[g, pl.ds(pl.multiple_of(at["t"] * feat, feat), feat), :]
        copies.append(pltpu.make_async_copy(src, basis.at[g], basis_sem.at[g]))
    for h, core in enumerate((1 - at["core"], at["core"])):
        src = inputs_ref.at[pl.ds(pl.multiple_of(core * half, half), half), :]
        copies.append(pltpu.make_async_copy(src, rows.at[h], row_sem.at[h]))
    for copy in copies:
        copy.start()
    for copy in copies[:n_g]:
        copy.wait()
    both = jnp.concatenate([basis[g] for g in range(n_g)], axis=1)
    for h in range(2):
        copies[n_g + h].wait()
        for k in range(NX):
            src = pl.multiple_of((at["x"] ^ k) * piece, piece)
            product = jnp.dot(rows[h, pl.ds(src, piece), :], both, preferred_element_type=F32)
            to = slice(k * piece, (k + 1) * piece)
            if h == 0:
                send_ref[to, :] = product.astype(BF16)
            else:
                own_ref[to, :] = product


def project(inputs, basis):
    tokens, feat = inputs.shape
    n_g, _, rank = basis.shape
    half = tokens // 2
    return pl.pallas_call(
        project_kernel,
        in_specs=[HBM] * 2,
        out_specs=[VMEM] * 2,
        out_shape=[
            jax.ShapeDtypeStruct((half, n_g * rank), BF16),
            jax.ShapeDtypeStruct((half, n_g * rank), F32),
        ],
        scratch_shapes=[
            pltpu.VMEM((2, half, feat), BF16),
            pltpu.VMEM((n_g, feat, rank), BF16),
            pltpu.SemaphoreType.DMA((2,)),
            pltpu.SemaphoreType.DMA((n_g,)),
        ],
        compiler_params=params(52),
        cost_estimate=cost(2 * tokens * feat * n_g * rank, 2 * tokens * feat),
        name="project",
    )(inputs, basis)


def stage_kernel(g, src_ref, dst_ref, sem):
    copy = pltpu.make_async_copy(src_ref.at[g], dst_ref, sem)
    copy.start()
    copy.wait()


def stage(stack, g):
    return pl.pallas_call(
        lambda *refs: stage_kernel(g, *refs),
        in_specs=[HBM],
        out_specs=VMEM,
        out_shape=jax.ShapeDtypeStruct(stack.shape[1:], stack.dtype),
        scratch_shapes=[pltpu.SemaphoreType.DMA],
        compiler_params=params(STAGE_MIB),
        cost_estimate=cost(0, 2 * 2 * stack.shape[1] * stack.shape[2]),
        name="stage",
    )(stack)


def half_product(at, core, part_ref, grad_ref, proj, g):
    half = part_ref.shape[0]
    piece = half // NX
    rank = proj.shape[1]
    for i, k in enumerate(PIECES):
        to = pl.multiple_of((at["x"] ^ k) * piece, piece)
        proj[pl.ds(to, piece), :] = part_ref[
            i * piece : (i + 1) * piece, g * rank : (g + 1) * rank
        ]
    tokens = pl.ds(pl.multiple_of(core * half, half), half)
    return jnp.dot(grad_ref[:, tokens], proj[...], preferred_element_type=F32)


def near_kernel(part_ref, *refs):
    grads, total_ref, proj = refs[:-2], refs[-2], refs[-1]
    at = place()
    for g, grad_ref in enumerate(grads):
        total_ref[g] = half_product(at, at["core"], part_ref, grad_ref, proj.at[g], g)


def rank_near(part, grads, rank):
    cols, tokens = grads[0].shape
    n_g = len(grads)
    return pl.pallas_call(
        near_kernel,
        in_specs=[VMEM] * (1 + n_g),
        out_specs=VMEM,
        out_shape=jax.ShapeDtypeStruct((n_g, cols, rank), F32),
        scratch_shapes=[pltpu.VMEM((n_g, tokens // 2, rank), BF16)],
        compiler_params=params(8),
        cost_estimate=cost(n_g * tokens * cols * rank, 4 * 2**20),
        name="rank_near",
    )(part, *grads)


def far_kernel(g, part_ref, near_ref, grad_ref, own_ref, *refs):
    outs, proj, total = refs[:-2], refs[-2], refs[-1]
    at = place()
    share = own_ref.shape[0]
    total[...] = near_ref[g] + half_product(at, 1 - at["core"], part_ref, grad_ref, proj, g)
    for k in range(NY):
        mine = total[pl.ds(pl.multiple_of((at["y"] ^ k) * share, 8), share), :]
        if k == 0:
            own_ref[...] = mine
        else:
            outs[k - 1][...] = mine.astype(BF16)


def rank_far(part, near, grad, g):
    cols, tokens = grad.shape
    rank = near.shape[2]
    share = cols // NY
    return pl.pallas_call(
        lambda *refs: far_kernel(g, *refs),
        in_specs=[VMEM] * 3,
        out_specs=[VMEM] * NY,
        out_shape=[jax.ShapeDtypeStruct((share, rank), F32)]
        + [jax.ShapeDtypeStruct((share, rank), BF16)] * (NY - 1),
        scratch_shapes=[pltpu.VMEM((tokens // 2, rank), BF16), pltpu.VMEM((cols, rank), F32)],
        compiler_params=params(8),
        cost_estimate=cost(tokens * cols * rank, 2 * 2**20),
        name="rank_far",
    )(part, near, grad)


def adam_kernel(n_g, *refs):
    owns, gots = refs[:n_g], refs[n_g : 2 * n_g]
    near_ref, far_ref, norm_ref = refs[2 * n_g :]
    low = place()["z"] == 0
    half = owns[0].shape[0] // 2
    for g in range(n_g):
        grad = owns[g][...] + gots[g][...].astype(F32)

        def moment(i):
            rows = slice((i * n_g + g) * half, (i * n_g + g + 1) * half)
            near, far = near_ref[rows, :], far_ref[rows, :]
            return jnp.concatenate(
                [jnp.where(low, near, far), jnp.where(low, far, near)], axis=0
            )

        new_first = beta_one * moment(0) + (1.0 - beta_one) * grad
        new_second = beta_two * moment(1) + (1.0 - beta_two) * grad * grad
        norm_ref[g] = (
            new_first / corr_one / (jnp.sqrt(new_second / corr_two) + epsilon)
        ).astype(BF16)


def adam(owns, gots, moments, far_moments):
    n_g = len(owns)
    share, rank = owns[0].shape
    return pl.pallas_call(
        lambda *refs: adam_kernel(n_g, *refs),
        in_specs=[VMEM] * (2 * n_g + 2),
        out_specs=VMEM,
        out_shape=jax.ShapeDtypeStruct((n_g, share, rank), BF16),
        compiler_params=params(8),
        name="adam",
    )(*owns, *gots, moments, far_moments)


def moments_kernel(n_g, *refs):
    owns, gots = refs[:n_g], refs[n_g : 2 * n_g]
    near_ref, new_first_ref, new_second_ref = refs[2 * n_g :]
    low = place()["z"] == 0
    half = owns[0].shape[0] // 2
    for g in range(n_g):
        grad = owns[g][...] + gots[g][...].astype(F32)
        grad = jnp.where(low, grad[:half], grad[half:])
        rows = slice(g * half, (g + 1) * half)
        first = near_ref[rows, :]
        second = near_ref[slice((n_g + g) * half, (n_g + g + 1) * half), :]
        new_first_ref[rows, 0, :] = beta_one * first + (1.0 - beta_one) * grad
        new_second_ref[rows, 0, :] = beta_two * second + (1.0 - beta_two) * grad * grad


def new_moments(owns, gots, moments):
    n_g = len(owns)
    share, rank = owns[0].shape
    return pl.pallas_call(
        lambda *refs: moments_kernel(n_g, *refs),
        in_specs=[VMEM] * (2 * n_g + 1),
        out_specs=[VMEM] * 2,
        out_shape=[jax.ShapeDtypeStruct((n_g * share // 2, 1, rank), F32)] * 2,
        compiler_params=params(8),
        name="new_moments",
    )(*owns, *gots, moments)


FIRST, REST = 336, 352


def update_kernel(windows, n, *refs):
    pieces, basis_ref = refs[:n], refs[n]
    out_ref, wide, norm, block, sem = refs[-5:]
    y = place()["y"]
    n_g, share, _ = pieces[0].shape
    copies = []
    for w, (own_pair, which) in enumerate(windows):
        pair = y >> 1 if own_pair else 1 - (y >> 1)
        parity = y & 1
        size = FIRST if len(which) == 1 else REST
        start = parity * REST if len(which) == 1 else (1 - parity) * FIRST
        for g in range(n_g):
            for i, at in zip(which, (parity, 1 - parity)):
                to = pl.ds(pl.multiple_of(at * share, 8), share)
                wide[w, g, to, :] = pieces[i][g].astype(F32)
            norm[w, g, :size, :] = wide[
                w, g, pl.ds(pl.multiple_of(start, 16), size), :
            ].astype(BF16)
            block[w, g, :size, :] = jnp.dot(
                norm[w, g, :size, :], basis_ref[g], preferred_element_type=F32
            ).astype(BF16)
            to = pl.ds(pl.multiple_of(pair * (2 * share) + start, 16), size)
            copies.append(
                pltpu.make_async_copy(
                    block.at[w, g, :size, :], out_ref.at[g, to, :], sem.at[w, g]
                )
            )
            copies[-1].start()
    for copy in copies:
        copy.wait()


def update(windows, pieces, basis_t, out):
    n, n_w = len(pieces), len(windows)
    n_g, share, rank = pieces[0].shape
    weight_rows = basis_t.shape[2]
    return pl.pallas_call(
        lambda *refs: update_kernel(windows, n, *refs),
        in_specs=[VMEM] * (n + 1) + ([HBM] if out is not None else []),
        out_specs=HBM,
        out_shape=jax.ShapeDtypeStruct((n_g, share * NY, weight_rows), BF16),
        scratch_shapes=[
            pltpu.VMEM((n_w, n_g, 2 * share, rank), F32),
            pltpu.VMEM((n_w, n_g, REST, rank), BF16),
            pltpu.VMEM((n_w, n_g, REST, weight_rows), BF16),
            pltpu.SemaphoreType.DMA((n_w, n_g)),
        ],
        input_output_aliases={} if out is None else {n + 1: 0},
        compiler_params=params(12),
        cost_estimate=cost(
            2 * n_w * n_g * REST * rank * weight_rows, 2 * n_w * n_g * REST * weight_rows
        ),
        name="update",
    )(*pieces, basis_t, *([] if out is None else [out]))


def body(inputs, grad_out, basis, first_moment, second_moment):
    weight_rows = basis.shape[1] // lax.axis_size("dp")
    row_basis = lax.dynamic_slice_in_dim(
        basis, lax.axis_index("dp") * weight_rows, weight_rows, 1
    )
    row_basis_t = jnp.transpose(row_basis, (0, 2, 1))
    piece = inputs.shape[0] // (2 * NX)
    grad_t = jnp.transpose(grad_out, (0, 2, 1))
    n_g, rank = first_moment.shape[:2]
    flat = lambda m: jnp.transpose(m, (0, 3, 2, 1)).reshape(-1, rank)
    send, own = project(inputs, basis)
    send, first, second = lax.optimization_barrier(
        (send, flat(first_moment), flat(second_moment))
    )
    moments = jnp.concatenate([first, second], axis=0)
    got = to_core(send)
    part = lambda v, k: v[k * piece : (k + 1) * piece].astype(F32)
    sums = [part(own, k) + part(got, k) for k in range(NX)]
    sums[0], grad_a = lax.optimization_barrier((sums[0], grad_t))
    total = sums[0]
    for k in ORDER:
        total = total + to_x(sums[k].astype(BF16), k).astype(F32)
    grads = [stage(grad_a, 0)]
    total, moments, row_basis_t, grads[0] = lax.optimization_barrier(
        (total, moments, row_basis_t, grads[0])
    )
    got = to_zlo(total.astype(BF16))
    far_moments = to_zhi(moments)
    total = (total + got.astype(F32)).astype(BF16)
    total, grad_b = lax.optimization_barrier((total, grad_t))
    parts = {0: total}
    for k in AG_X:
        parts[k] = to_x(total, k)
    near_part = jnp.concatenate([parts[k] for k in PIECES], axis=0)
    near_part, grad, far_moments = lax.optimization_barrier(
        (near_part, stage(grad_b, 1), far_moments)
    )
    grads.append(grad)
    far_part = to_core(near_part)
    near = rank_near(near_part, grads, rank)
    far_part, near = lax.optimization_barrier((far_part, near))

    owns, gots = [], []
    for g in range(n_g):
        own, *others = rank_far(far_part, near, grads[g], g)
        for k in ORDER:
            own = own + to_y(others[k - 1], k).astype(F32)
        owns.append(own)
        gots.append(to_zhi(own.astype(BF16)))
    norm = adam(owns, gots, moments, far_moments)
    pieces = {k: to_y(norm, k) for k in AG_Y}
    out = update([(True, (0,))], [norm], row_basis_t, None)
    new_first, new_second = new_moments(owns, gots, moments)
    out = update([(False, (0,))], [pieces[2]], row_basis_t, out)
    out = update(
        [(True, (0, 1)), (False, (2, 3))],
        [norm, pieces[1], pieces[2], pieces[3]],
        row_basis_t,
        out,
    )

    def shaped(m):
        return jnp.transpose(m.reshape(n_g, -1, 1, rank), (0, 3, 2, 1))

    return jnp.transpose(out, (0, 2, 1)), shaped(new_first), shaped(new_second)


def solution(mesh):
    in_specs = (
        P("dp", "tensor"),
        P(None, "dp", "tensor"),
        P(),
        P(None, None, "tensor", "dp"),
        P(None, None, "tensor", "dp"),
    )
    out_specs = (
        P(None, "dp", "tensor"),
        P(None, None, "tensor", "dp"),
        P(None, None, "tensor", "dp"),
    )
    return jax.shard_map(body, mesh=mesh, in_specs=in_specs, out_specs=out_specs, check_vma=False)
```

```python
import jax
import jax.numpy as jnp
from jax import lax
from jax.experimental import pallas as pl
from jax.experimental.pallas import tpu as pltpu
from jax.sharding import PartitionSpec as P

STEP = 10

beta_one = 0.9
beta_two = 0.999
epsilon = 1e-08
corr_one = 1.0 - beta_one**STEP
corr_two = 1.0 - beta_two**STEP

NX, NY = 4, 4
ORDER = (2, 1, 3)
STAGE_MIB = 48
AG_X, AG_Y = (2, 1, 3), (2, 1, 3)
PIECES = (0, 1, 3, 2)

F32, BF16 = jnp.float32, jnp.bfloat16
HBM = pl.BlockSpec(memory_space=pltpu.HBM)
VMEM = pl.BlockSpec(memory_space=pltpu.VMEM)


def swap(v, axis, size, bits):
    return lax.ppermute(v, axis, [(i, i ^ bits) for i in range(size)])


def to_core(v):
    return swap(v, "tensor", 16, 1)


def to_x(v, k):
    return swap(v, "tensor", 16, k * 2)


def to_zlo(v):
    return swap(v, "tensor", 16, 8)


def to_y(v, k):
    return swap(v, "dp", 8, k * 2)


def to_zhi(v):
    return swap(v, "dp", 8, 1)


def place():
    t, d = lax.axis_index("tensor"), lax.axis_index("dp")
    return {"t": t, "core": t & 1, "x": (t >> 1) & 3, "y": d >> 1, "z": d & 1}


def params(mib):
    return pltpu.CompilerParams(vmem_limit_bytes=mib * 2**20)


def cost(flops, moved):
    return pl.CostEstimate(flops=flops, bytes_accessed=moved, transcendentals=0)


def project_kernel(
    inputs_ref, basis_ref, send_ref, own_ref, rows, basis, row_sem, basis_sem
):
    at = place()
    n_g, feat, rank = basis.shape
    half = rows.shape[1]
    piece = half // NX
    src = basis_ref.at[:, pl.ds(pl.multiple_of(at["t"] * feat, feat), feat), :]
    copies = [pltpu.make_async_copy(src, basis, basis_sem)]
    for h, core in enumerate((1 - at["core"], at["core"])):
        src = inputs_ref.at[pl.ds(pl.multiple_of(core * half, half), half), :]
        copies.append(pltpu.make_async_copy(src, rows.at[h], row_sem.at[h]))
    for copy in copies:
        copy.start()
    copies[0].wait()
    both = jnp.concatenate([basis[g] for g in range(n_g)], axis=1)
    for h in range(2):
        copies[1 + h].wait()
        for k in range(NX):
            src = pl.multiple_of((at["x"] ^ k) * piece, piece)
            product = jnp.dot(rows[h, pl.ds(src, piece), :], both, preferred_element_type=F32)
            to = slice(k * piece, (k + 1) * piece)
            if h == 0:
                send_ref[to, :] = product.astype(BF16)
            else:
                own_ref[to, :] = product


def project(inputs, basis):
    tokens, feat = inputs.shape
    n_g, _, rank = basis.shape
    half = tokens // 2
    return pl.pallas_call(
        project_kernel,
        in_specs=[HBM] * 2,
        out_specs=[VMEM] * 2,
        out_shape=[
            jax.ShapeDtypeStruct((half, n_g * rank), BF16),
            jax.ShapeDtypeStruct((half, n_g * rank), F32),
        ],
        scratch_shapes=[
            pltpu.VMEM((2, half, feat), BF16),
            pltpu.VMEM((n_g, feat, rank), BF16),
            pltpu.SemaphoreType.DMA((2,)),
            pltpu.SemaphoreType.DMA,
        ],
        compiler_params=params(52),
        cost_estimate=cost(2 * tokens * feat * n_g * rank, 2 * tokens * feat),
        name="project",
    )(inputs, basis)


def stage_kernel(g, src_ref, dst_ref, sem):
    copy = pltpu.make_async_copy(src_ref.at[g], dst_ref, sem)
    copy.start()
    copy.wait()


def stage(stack, g):
    return pl.pallas_call(
        lambda *refs: stage_kernel(g, *refs),
        in_specs=[HBM],
        out_specs=VMEM,
        out_shape=jax.ShapeDtypeStruct(stack.shape[1:], stack.dtype),
        scratch_shapes=[pltpu.SemaphoreType.DMA],
        compiler_params=params(STAGE_MIB),
        cost_estimate=cost(0, 2 * 2 * stack.shape[1] * stack.shape[2]),
        name="stage",
    )(stack)


def half_product(at, core, part_ref, grad_ref, proj, g):
    half = part_ref.shape[0]
    piece = half // NX
    rank = proj.shape[1]
    for i, k in enumerate(PIECES):
        to = pl.multiple_of((at["x"] ^ k) * piece, piece)
        proj[pl.ds(to, piece), :] = part_ref[
            i * piece : (i + 1) * piece, g * rank : (g + 1) * rank
        ]
    tokens = pl.ds(pl.multiple_of(core * half, half), half)
    return jnp.dot(grad_ref[:, tokens], proj[...], preferred_element_type=F32)


def near_kernel(part_ref, *refs):
    grads, total_ref, proj = refs[:-2], refs[-2], refs[-1]
    at = place()
    for g, grad_ref in enumerate(grads):
        total_ref[g] = half_product(at, at["core"], part_ref, grad_ref, proj.at[g], g)


def rank_near(part, grads, rank):
    cols, tokens = grads[0].shape
    n_g = len(grads)
    return pl.pallas_call(
        near_kernel,
        in_specs=[VMEM] * (1 + n_g),
        out_specs=VMEM,
        out_shape=jax.ShapeDtypeStruct((n_g, cols, rank), F32),
        scratch_shapes=[pltpu.VMEM((n_g, tokens // 2, rank), BF16)],
        compiler_params=params(8),
        cost_estimate=cost(n_g * tokens * cols * rank, 4 * 2**20),
        name="rank_near",
    )(part, *grads)


def far_kernel(g, part_ref, near_ref, grad_ref, own_ref, *refs):
    outs, proj, total = refs[:-2], refs[-2], refs[-1]
    at = place()
    share = own_ref.shape[0]
    total[...] = near_ref[g] + half_product(at, 1 - at["core"], part_ref, grad_ref, proj, g)
    for k in range(NY):
        mine = total[pl.ds(pl.multiple_of((at["y"] ^ k) * share, 8), share), :]
        if k == 0:
            own_ref[...] = mine
        else:
            outs[k - 1][...] = mine.astype(BF16)


def rank_far(part, near, grad, g):
    cols, tokens = grad.shape
    rank = near.shape[2]
    share = cols // NY
    return pl.pallas_call(
        lambda *refs: far_kernel(g, *refs),
        in_specs=[VMEM] * 3,
        out_specs=[VMEM] * NY,
        out_shape=[jax.ShapeDtypeStruct((share, rank), F32)]
        + [jax.ShapeDtypeStruct((share, rank), BF16)] * (NY - 1),
        scratch_shapes=[pltpu.VMEM((tokens // 2, rank), BF16), pltpu.VMEM((cols, rank), F32)],
        compiler_params=params(8),
        cost_estimate=cost(tokens * cols * rank, 2 * 2**20),
        name="rank_far",
    )(part, near, grad)


def adam_kernel(n_g, *refs):
    owns, gots = refs[:n_g], refs[n_g : 2 * n_g]
    near_ref, far_ref, norm_ref = refs[2 * n_g :]
    low = place()["z"] == 0
    half = owns[0].shape[0] // 2
    for g in range(n_g):
        grad = owns[g][...] + gots[g][...].astype(F32)

        def moment(i):
            rows = slice((i * n_g + g) * half, (i * n_g + g + 1) * half)
            near, far = near_ref[rows, :], far_ref[rows, :]
            return jnp.concatenate(
                [jnp.where(low, near, far), jnp.where(low, far, near)], axis=0
            )

        new_first = beta_one * moment(0) + (1.0 - beta_one) * grad
        new_second = beta_two * moment(1) + (1.0 - beta_two) * grad * grad
        norm_ref[g] = (
            new_first / corr_one / (jnp.sqrt(new_second / corr_two) + epsilon)
        ).astype(BF16)


def adam(owns, gots, moments, far_moments):
    n_g = len(owns)
    share, rank = owns[0].shape
    return pl.pallas_call(
        lambda *refs: adam_kernel(n_g, *refs),
        in_specs=[VMEM] * (2 * n_g + 2),
        out_specs=VMEM,
        out_shape=jax.ShapeDtypeStruct((n_g, share, rank), BF16),
        compiler_params=params(8),
        name="adam",
    )(*owns, *gots, moments, far_moments)


def moments_kernel(n_g, *refs):
    owns, gots = refs[:n_g], refs[n_g : 2 * n_g]
    near_ref, new_first_ref, new_second_ref = refs[2 * n_g :]
    low = place()["z"] == 0
    half = owns[0].shape[0] // 2
    for g in range(n_g):
        grad = owns[g][...] + gots[g][...].astype(F32)
        grad = jnp.where(low, grad[:half], grad[half:])
        rows = slice(g * half, (g + 1) * half)
        first = near_ref[rows, :]
        second = near_ref[slice((n_g + g) * half, (n_g + g + 1) * half), :]
        new_first_ref[rows, 0, :] = beta_one * first + (1.0 - beta_one) * grad
        new_second_ref[rows, 0, :] = beta_two * second + (1.0 - beta_two) * grad * grad


def new_moments(owns, gots, moments):
    n_g = len(owns)
    share, rank = owns[0].shape
    return pl.pallas_call(
        lambda *refs: moments_kernel(n_g, *refs),
        in_specs=[VMEM] * (2 * n_g + 1),
        out_specs=[VMEM] * 2,
        out_shape=[jax.ShapeDtypeStruct((n_g * share // 2, 1, rank), F32)] * 2,
        compiler_params=params(8),
        name="new_moments",
    )(*owns, *gots, moments)


FIRST, REST = 336, 352


def update_kernel(windows, n, *refs):
    pieces, basis_ref = refs[:n], refs[n]
    out_ref, wide, norm, block, sem = refs[-5:]
    y = place()["y"]
    n_g, share, _ = pieces[0].shape
    copies = []
    for w, (own_pair, which) in enumerate(windows):
        pair = y >> 1 if own_pair else 1 - (y >> 1)
        parity = y & 1
        size = FIRST if len(which) == 1 else REST
        start = parity * REST if len(which) == 1 else (1 - parity) * FIRST
        for g in range(n_g):
            for i, at in zip(which, (parity, 1 - parity)):
                to = pl.ds(pl.multiple_of(at * share, 8), share)
                wide[w, g, to, :] = pieces[i][g].astype(F32)
            norm[w, g, :size, :] = wide[
                w, g, pl.ds(pl.multiple_of(start, 16), size), :
            ].astype(BF16)
            for c, (low, high) in enumerate(((0, 176), (176, size))):
                block[w, g, low:high, :] = jnp.dot(
                    norm[w, g, low:high, :], basis_ref[g], preferred_element_type=F32
                ).astype(BF16)
                at_row = pl.multiple_of(pair * (2 * share) + start + low, 16)
                copies.append(
                    pltpu.make_async_copy(
                        block.at[w, g, low:high, :],
                        out_ref.at[g, pl.ds(at_row, high - low), :],
                        sem.at[w, g, c],
                    )
                )
                copies[-1].start()
    for copy in copies:
        copy.wait()


def update(windows, pieces, basis_t, out):
    n, n_w = len(pieces), len(windows)
    n_g, share, rank = pieces[0].shape
    weight_rows = basis_t.shape[2]
    return pl.pallas_call(
        lambda *refs: update_kernel(windows, n, *refs),
        in_specs=[VMEM] * (n + 1) + ([HBM] if out is not None else []),
        out_specs=HBM,
        out_shape=jax.ShapeDtypeStruct((n_g, share * NY, weight_rows), BF16),
        scratch_shapes=[
            pltpu.VMEM((n_w, n_g, 2 * share, rank), F32),
            pltpu.VMEM((n_w, n_g, REST, rank), BF16),
            pltpu.VMEM((n_w, n_g, REST, weight_rows), BF16),
            pltpu.SemaphoreType.DMA((n_w, n_g, 2)),
        ],
        input_output_aliases={} if out is None else {n + 1: 0},
        compiler_params=params(12),
        cost_estimate=cost(
            2 * n_w * n_g * REST * rank * weight_rows, 2 * n_w * n_g * REST * weight_rows
        ),
        name="update",
    )(*pieces, basis_t, *([] if out is None else [out]))


def body(inputs, grad_out, basis, first_moment, second_moment):
    weight_rows = basis.shape[1] // lax.axis_size("dp")
    row_basis = lax.dynamic_slice_in_dim(
        basis, lax.axis_index("dp") * weight_rows, weight_rows, 1
    )
    row_basis_t = jnp.transpose(row_basis, (0, 2, 1))
    piece = inputs.shape[0] // (2 * NX)
    grad_t = jnp.transpose(grad_out, (0, 2, 1))
    n_g, rank = first_moment.shape[:2]
    flat = lambda m: jnp.transpose(m, (0, 3, 2, 1)).reshape(-1, rank)
    send, own = project(inputs, basis)
    send, first, second = lax.optimization_barrier(
        (send, flat(first_moment), flat(second_moment))
    )
    moments = jnp.concatenate([first, second], axis=0)
    got = to_core(send)
    part = lambda v, k: v[k * piece : (k + 1) * piece].astype(F32)
    sums = [part(own, k) + part(got, k) for k in range(NX)]
    sums[0], grad_a = lax.optimization_barrier((sums[0], grad_t))
    total = sums[0]
    for k in ORDER:
        total = total + to_x(sums[k].astype(BF16), k).astype(F32)
    grads = [stage(grad_a, 0)]
    total, moments, row_basis_t, grads[0] = lax.optimization_barrier(
        (total, moments, row_basis_t, grads[0])
    )
    got = to_zlo(total.astype(BF16))
    far_moments = to_zhi(moments)
    total = (total + got.astype(F32)).astype(BF16)
    total, grad_b = lax.optimization_barrier((total, grad_t))
    parts = {0: total}
    for k in AG_X:
        parts[k] = to_x(total, k)
    near_part = jnp.concatenate([parts[k] for k in PIECES], axis=0)
    near_part, grad, far_moments = lax.optimization_barrier(
        (near_part, stage(grad_b, 1), far_moments)
    )
    grads.append(grad)
    far_part = to_core(near_part)
    near = rank_near(near_part, grads, rank)
    far_part, near = lax.optimization_barrier((far_part, near))

    owns, gots = [], []
    for g in range(n_g):
        own, *others = rank_far(far_part, near, grads[g], g)
        for k in ORDER:
            own = own + to_y(others[k - 1], k).astype(F32)
        owns.append(own)
        gots.append(to_zhi(own.astype(BF16)))
    norm = adam(owns, gots, moments, far_moments)
    pieces = {k: to_y(norm, k) for k in AG_Y}
    out = update([(True, (0,))], [norm], row_basis_t, None)
    new_first, new_second = new_moments(owns, gots, moments)
    out = update([(False, (0,))], [pieces[2]], row_basis_t, out)
    out = update(
        [(True, (0, 1)), (False, (2, 3))],
        [norm, pieces[1], pieces[2], pieces[3]],
        row_basis_t,
        out,
    )

    def shaped(m):
        return jnp.transpose(m.reshape(n_g, -1, 1, rank), (0, 3, 2, 1))

    return jnp.transpose(out, (0, 2, 1)), shaped(new_first), shaped(new_second)


def solution(mesh):
    in_specs = (
        P("dp", "tensor"),
        P(None, "dp", "tensor"),
        P(),
        P(None, None, "tensor", "dp"),
        P(None, None, "tensor", "dp"),
    )
    out_specs = (
        P(None, "dp", "tensor"),
        P(None, None, "tensor", "dp"),
        P(None, None, "tensor", "dp"),
    )
    return jax.shard_map(body, mesh=mesh, in_specs=in_specs, out_specs=out_specs, check_vma=False)
```

```python
import jax
import jax.numpy as jnp
from jax import lax
from jax.experimental import pallas as pl
from jax.experimental.pallas import tpu as pltpu
from jax.sharding import PartitionSpec as P

STEP = 10

beta_one = 0.9
beta_two = 0.999
epsilon = 1e-08
corr_one = 1.0 - beta_one**STEP
corr_two = 1.0 - beta_two**STEP

NX, NY = 4, 4
ORDER_X, ORDER_Y = (1, 2, 3), (2, 1, 3)
STAGE_MIB = 48
AG_X, AG_Y = (2, 1, 3), (2, 1, 3)
PIECES = (0, 1, 3, 2)

F32, BF16 = jnp.float32, jnp.bfloat16
HBM = pl.BlockSpec(memory_space=pltpu.HBM)
VMEM = pl.BlockSpec(memory_space=pltpu.VMEM)


def swap(v, axis, size, bits):
    return lax.ppermute(v, axis, [(i, i ^ bits) for i in range(size)])


def to_core(v):
    return swap(v, "tensor", 16, 1)


def to_x(v, k):
    return swap(v, "tensor", 16, k * 2)


def to_zlo(v):
    return swap(v, "tensor", 16, 8)


def to_y(v, k):
    return swap(v, "dp", 8, k * 2)


def to_zhi(v):
    return swap(v, "dp", 8, 1)


def place():
    t, d = lax.axis_index("tensor"), lax.axis_index("dp")
    return {"t": t, "core": t & 1, "x": (t >> 1) & 3, "y": d >> 1, "z": d & 1}


def params(mib):
    return pltpu.CompilerParams(vmem_limit_bytes=mib * 2**20)


def cost(flops, moved):
    return pl.CostEstimate(flops=flops, bytes_accessed=moved, transcendentals=0)


def project_kernel(
    inputs_ref, basis_ref, send_ref, own_ref, rows, basis, row_sem, basis_sem
):
    at = place()
    n_g, feat, rank = basis.shape
    half = rows.shape[1]
    piece = half // NX
    src = basis_ref.at[:, pl.ds(pl.multiple_of(at["t"] * feat, feat), feat), :]
    copies = [pltpu.make_async_copy(src, basis, basis_sem)]
    for h, core in enumerate((1 - at["core"], at["core"])):
        src = inputs_ref.at[pl.ds(pl.multiple_of(core * half, half), half), :]
        copies.append(pltpu.make_async_copy(src, rows.at[h], row_sem.at[h]))
    for copy in copies:
        copy.start()
    copies[0].wait()
    both = jnp.concatenate([basis[g] for g in range(n_g)], axis=1)
    for h in range(2):
        copies[1 + h].wait()
        for k in range(NX):
            src = pl.multiple_of((at["x"] ^ k) * piece, piece)
            product = jnp.dot(rows[h, pl.ds(src, piece), :], both, preferred_element_type=F32)
            to = slice(k * piece, (k + 1) * piece)
            if h == 0:
                send_ref[to, :] = product.astype(BF16)
            else:
                own_ref[to, :] = product


def project(inputs, basis):
    tokens, feat = inputs.shape
    n_g, _, rank = basis.shape
    half = tokens // 2
    return pl.pallas_call(
        project_kernel,
        in_specs=[HBM] * 2,
        out_specs=[VMEM] * 2,
        out_shape=[
            jax.ShapeDtypeStruct((half, n_g * rank), BF16),
            jax.ShapeDtypeStruct((half, n_g * rank), F32),
        ],
        scratch_shapes=[
            pltpu.VMEM((2, half, feat), BF16),
            pltpu.VMEM((n_g, feat, rank), BF16),
            pltpu.SemaphoreType.DMA((2,)),
            pltpu.SemaphoreType.DMA,
        ],
        compiler_params=params(52),
        cost_estimate=cost(2 * tokens * feat * n_g * rank, 2 * tokens * feat),
        name="project",
    )(inputs, basis)


def stage_kernel(g, src_ref, dst_ref, sem):
    copy = pltpu.make_async_copy(src_ref.at[g], dst_ref, sem)
    copy.start()
    copy.wait()


def stage(stack, g):
    return pl.pallas_call(
        lambda *refs: stage_kernel(g, *refs),
        in_specs=[HBM],
        out_specs=VMEM,
        out_shape=jax.ShapeDtypeStruct(stack.shape[1:], stack.dtype),
        scratch_shapes=[pltpu.SemaphoreType.DMA],
        compiler_params=params(STAGE_MIB),
        cost_estimate=cost(0, 2 * 2 * stack.shape[1] * stack.shape[2]),
        name="stage",
    )(stack)


def half_product(at, core, part_ref, grad_ref, proj, g):
    half = part_ref.shape[0]
    piece = half // NX
    rank = proj.shape[1]
    for i, k in enumerate(PIECES):
        to = pl.multiple_of((at["x"] ^ k) * piece, piece)
        proj[pl.ds(to, piece), :] = part_ref[
            i * piece : (i + 1) * piece, g * rank : (g + 1) * rank
        ]
    tokens = pl.ds(pl.multiple_of(core * half, half), half)
    return jnp.dot(grad_ref[:, tokens], proj[...], preferred_element_type=F32)


def near_kernel(part_ref, *refs):
    grads, total_ref, proj = refs[:-2], refs[-2], refs[-1]
    at = place()
    for g, grad_ref in enumerate(grads):
        total_ref[g] = half_product(at, at["core"], part_ref, grad_ref, proj.at[g], g)


def rank_near(part, grads, rank):
    cols, tokens = grads[0].shape
    n_g = len(grads)
    return pl.pallas_call(
        near_kernel,
        in_specs=[VMEM] * (1 + n_g),
        out_specs=VMEM,
        out_shape=jax.ShapeDtypeStruct((n_g, cols, rank), F32),
        scratch_shapes=[pltpu.VMEM((n_g, tokens // 2, rank), BF16)],
        compiler_params=params(8),
        cost_estimate=cost(n_g * tokens * cols * rank, 4 * 2**20),
        name="rank_near",
    )(part, *grads)


def far_kernel(g, part_ref, near_ref, grad_ref, own_ref, *refs):
    outs, proj, total = refs[:-2], refs[-2], refs[-1]
    at = place()
    share = own_ref.shape[0]
    total[...] = near_ref[g] + half_product(at, 1 - at["core"], part_ref, grad_ref, proj, g)
    for k in range(NY):
        mine = total[pl.ds(pl.multiple_of((at["y"] ^ k) * share, 8), share), :]
        if k == 0:
            own_ref[...] = mine
        else:
            outs[k - 1][...] = mine.astype(BF16)


def rank_far(part, near, grad, g):
    cols, tokens = grad.shape
    rank = near.shape[2]
    share = cols // NY
    return pl.pallas_call(
        lambda *refs: far_kernel(g, *refs),
        in_specs=[VMEM] * 3,
        out_specs=[VMEM] * NY,
        out_shape=[jax.ShapeDtypeStruct((share, rank), F32)]
        + [jax.ShapeDtypeStruct((share, rank), BF16)] * (NY - 1),
        scratch_shapes=[pltpu.VMEM((tokens // 2, rank), BF16), pltpu.VMEM((cols, rank), F32)],
        compiler_params=params(8),
        cost_estimate=cost(tokens * cols * rank, 2 * 2**20),
        name="rank_far",
    )(part, near, grad)


def adam_kernel(n_g, *refs):
    owns, gots = refs[:n_g], refs[n_g : 2 * n_g]
    near_ref, far_ref, norm_ref = refs[2 * n_g :]
    low = place()["z"] == 0
    half = owns[0].shape[0] // 2
    for g in range(n_g):
        grad = owns[g][...] + gots[g][...].astype(F32)

        def moment(i):
            rows = slice((i * n_g + g) * half, (i * n_g + g + 1) * half)
            near, far = near_ref[rows, :], far_ref[rows, :]
            return jnp.concatenate(
                [jnp.where(low, near, far), jnp.where(low, far, near)], axis=0
            )

        new_first = beta_one * moment(0) + (1.0 - beta_one) * grad
        new_second = beta_two * moment(1) + (1.0 - beta_two) * grad * grad
        norm_ref[g] = (
            new_first / corr_one / (jnp.sqrt(new_second / corr_two) + epsilon)
        ).astype(BF16)


def adam(owns, gots, moments, far_moments):
    n_g = len(owns)
    share, rank = owns[0].shape
    return pl.pallas_call(
        lambda *refs: adam_kernel(n_g, *refs),
        in_specs=[VMEM] * (2 * n_g + 2),
        out_specs=VMEM,
        out_shape=jax.ShapeDtypeStruct((n_g, share, rank), BF16),
        compiler_params=params(8),
        name="adam",
    )(*owns, *gots, moments, far_moments)


def moments_kernel(n_g, *refs):
    owns, gots = refs[:n_g], refs[n_g : 2 * n_g]
    near_ref, new_first_ref, new_second_ref = refs[2 * n_g :]
    low = place()["z"] == 0
    half = owns[0].shape[0] // 2
    for g in range(n_g):
        grad = owns[g][...] + gots[g][...].astype(F32)
        grad = jnp.where(low, grad[:half], grad[half:])
        rows = slice(g * half, (g + 1) * half)
        first = near_ref[rows, :]
        second = near_ref[slice((n_g + g) * half, (n_g + g + 1) * half), :]
        new_first_ref[rows, 0, :] = beta_one * first + (1.0 - beta_one) * grad
        new_second_ref[rows, 0, :] = beta_two * second + (1.0 - beta_two) * grad * grad


def new_moments(owns, gots, moments):
    n_g = len(owns)
    share, rank = owns[0].shape
    return pl.pallas_call(
        lambda *refs: moments_kernel(n_g, *refs),
        in_specs=[VMEM] * (2 * n_g + 1),
        out_specs=[VMEM] * 2,
        out_shape=[jax.ShapeDtypeStruct((n_g * share // 2, 1, rank), F32)] * 2,
        compiler_params=params(8),
        name="new_moments",
    )(*owns, *gots, moments)


FIRST, REST = 336, 352


def update_kernel(windows, n, *refs):
    pieces, basis_ref = refs[:n], refs[n]
    out_ref, wide, norm, block, sem = refs[-5:]
    y = place()["y"]
    n_g, share, _ = pieces[0].shape
    copies = []
    for w, (own_pair, which) in enumerate(windows):
        pair = y >> 1 if own_pair else 1 - (y >> 1)
        parity = y & 1
        size = FIRST if len(which) == 1 else REST
        start = parity * REST if len(which) == 1 else (1 - parity) * FIRST
        for g in range(n_g):
            for i, at in zip(which, (parity, 1 - parity)):
                to = pl.ds(pl.multiple_of(at * share, 8), share)
                wide[w, g, to, :] = pieces[i][g].astype(F32)
            norm[w, g, :size, :] = wide[
                w, g, pl.ds(pl.multiple_of(start, 16), size), :
            ].astype(BF16)
            for c, (low, high) in enumerate(((0, 176), (176, size))):
                block[w, g, low:high, :] = jnp.dot(
                    norm[w, g, low:high, :], basis_ref[g], preferred_element_type=F32
                ).astype(BF16)
                at_row = pl.multiple_of(pair * (2 * share) + start + low, 16)
                copies.append(
                    pltpu.make_async_copy(
                        block.at[w, g, low:high, :],
                        out_ref.at[g, pl.ds(at_row, high - low), :],
                        sem.at[w, g, c],
                    )
                )
                copies[-1].start()
    for copy in copies:
        copy.wait()


def update(windows, pieces, basis_t, out):
    n, n_w = len(pieces), len(windows)
    n_g, share, rank = pieces[0].shape
    weight_rows = basis_t.shape[2]
    return pl.pallas_call(
        lambda *refs: update_kernel(windows, n, *refs),
        in_specs=[VMEM] * (n + 1) + ([HBM] if out is not None else []),
        out_specs=HBM,
        out_shape=jax.ShapeDtypeStruct((n_g, share * NY, weight_rows), BF16),
        scratch_shapes=[
            pltpu.VMEM((n_w, n_g, 2 * share, rank), F32),
            pltpu.VMEM((n_w, n_g, REST, rank), BF16),
            pltpu.VMEM((n_w, n_g, REST, weight_rows), BF16),
            pltpu.SemaphoreType.DMA((n_w, n_g, 2)),
        ],
        input_output_aliases={} if out is None else {n + 1: 0},
        compiler_params=params(12),
        cost_estimate=cost(
            2 * n_w * n_g * REST * rank * weight_rows, 2 * n_w * n_g * REST * weight_rows
        ),
        name="update",
    )(*pieces, basis_t, *([] if out is None else [out]))


def body(inputs, grad_out, basis, first_moment, second_moment):
    weight_rows = basis.shape[1] // lax.axis_size("dp")
    row_basis = lax.dynamic_slice_in_dim(
        basis, lax.axis_index("dp") * weight_rows, weight_rows, 1
    )
    row_basis_t = jnp.transpose(row_basis, (0, 2, 1))
    piece = inputs.shape[0] // (2 * NX)
    grad_t = jnp.transpose(grad_out, (0, 2, 1))
    n_g, rank = first_moment.shape[:2]
    flat = lambda m: jnp.transpose(m, (0, 3, 2, 1)).reshape(-1, rank)
    send, own = project(inputs, basis)
    send, first, second = lax.optimization_barrier(
        (send, flat(first_moment), flat(second_moment))
    )
    moments = jnp.concatenate([first, second], axis=0)
    got = to_core(send)
    part = lambda v, k: v[k * piece : (k + 1) * piece].astype(F32)
    sums = [part(own, k) + part(got, k) for k in range(NX)]
    sums[0], grad_a = lax.optimization_barrier((sums[0], grad_t))
    total = sums[0]
    for k in ORDER_X:
        total = total + to_x(sums[k].astype(BF16), k).astype(F32)
    grads = [stage(grad_a, 0)]
    total, moments, row_basis_t, grads[0] = lax.optimization_barrier(
        (total, moments, row_basis_t, grads[0])
    )
    got = to_zlo(total.astype(BF16))
    far_moments = to_zhi(moments)
    total = (total + got.astype(F32)).astype(BF16)
    total, grad_b = lax.optimization_barrier((total, grad_t))
    parts = {0: total}
    for k in AG_X:
        parts[k] = to_x(total, k)
    near_part = jnp.concatenate([parts[k] for k in PIECES], axis=0)
    near_part, grad, far_moments = lax.optimization_barrier(
        (near_part, stage(grad_b, 1), far_moments)
    )
    grads.append(grad)
    far_part = to_core(near_part)
    near = rank_near(near_part, grads, rank)
    far_part, near = lax.optimization_barrier((far_part, near))

    owns, gots = [], []
    for g in range(n_g):
        own, *others = rank_far(far_part, near, grads[g], g)
        for k in ORDER_Y:
            own = own + to_y(others[k - 1], k).astype(F32)
        owns.append(own)
        gots.append(to_zhi(own.astype(BF16)))
    norm = adam(owns, gots, moments, far_moments)
    pieces = {k: to_y(norm, k) for k in AG_Y}
    out = update([(True, (0,))], [norm], row_basis_t, None)
    new_first, new_second = new_moments(owns, gots, moments)
    out = update([(False, (0,))], [pieces[2]], row_basis_t, out)
    out = update(
        [(True, (0, 1)), (False, (2, 3))],
        [norm, pieces[1], pieces[2], pieces[3]],
        row_basis_t,
        out,
    )

    def shaped(m):
        return jnp.transpose(m.reshape(n_g, -1, 1, rank), (0, 3, 2, 1))

    return jnp.transpose(out, (0, 2, 1)), shaped(new_first), shaped(new_second)


def solution(mesh):
    in_specs = (
        P("dp", "tensor"),
        P(None, "dp", "tensor"),
        P(),
        P(None, None, "tensor", "dp"),
        P(None, None, "tensor", "dp"),
    )
    out_specs = (
        P(None, "dp", "tensor"),
        P(None, None, "tensor", "dp"),
        P(None, None, "tensor", "dp"),
    )
    return jax.shard_map(body, mesh=mesh, in_specs=in_specs, out_specs=out_specs, check_vma=False)
```
